32 devices in a mesh: tm: 4 (over x, core), site: 8 (over z, y).
Axes of the slice: x: 2, y: 2, z: 4, core: 2. Of those that a mesh axis runs over, the one named last changes fastest.
Arguments:
- source: float32 [16, 8, 6144], P('tm', None, 'site')
- aux_field: float32 [16, 6144], P('tm', 'site'), may hold values from -2 to 2
- hopping_exp: float32 [6144, 6144], P('site'), as said below
Outputs:
- solution_field: float32 [16, 8, 6144], P('tm', None, 'site')
- residual: float32 [16, 8, 6144], P('tm', None, 'site')
The draws below stay inside these ranges and needn't reach their ends.
Inputs may be any that keep to these rules, and one draw needn't show every extreme that they name: hopping_exp is exactly symmetric and positive definite.
All inputs are finite; a program needn't handle non-finite values.
Results may differ from the reference program's by a relative error of at most 0.00024.
Values sent between devices are 32-bit elements; how exact they have to be, the bound alone decides.
A program may use at most 64 MiB of HBM per device.

```python
import jax
import jax.numpy as jnp
from jax import lax

SITES = 6144
SOURCES = 8
ITERS = 2
SLICES = 16


def draw_source(key, part):
    key = jax.random.fold_in(key, 11)
    base_key = jax.random.fold_in(key, 0)
    slices = jnp.arange(SLICES, dtype=jnp.float32)
    ramp = 0.5 + slices / max(SLICES - 1, 1)
    base = jax.random.normal(base_key, (SLICES, SOURCES, SITES), jnp.float32)
    return (base * ramp[:, None, None]).astype(jnp.float32)


def draw_hopping_exp(key, part):
    key = jax.random.fold_in(key, 23)
    noise = jax.random.normal(key, (SITES, SITES), jnp.float32)
    factor = 0.25 / (2.0 * SITES) ** 0.5
    index = jnp.arange(SITES)
    identity = (index[:, None] == index[None, :]).astype(jnp.float32)
    return (identity + factor * (noise + noise.T)).astype(jnp.float32)


def levels(key, dims, cuts, low, largest):
    def one(position, shards_of):
        steps = jax.random.uniform(jax.random.fold_in(jax.random.fold_in(key, 6), position), (shards_of,), jnp.float32, low / len(cuts), largest / len(cuts))
        return jnp.repeat(jnp.exp(steps), dims[position] // shards_of).reshape((-1,) + (1,) * (len(dims) - position - 1))

    gain = one(*cuts[0])
    for cut in cuts[1:]:
        gain = gain * one(*cut)
    return gain


def normal_values(stream_key, extent, deviation, limit, cuts=(), held_as=jnp.bfloat16):
    array = jax.random.normal(stream_key, extent, jnp.float32) * deviation
    if len(cuts) > 0:
        array = levels(stream_key, extent, cuts, -0.22, 0.18) * array
    return jnp.clip(array, min=-limit, max=limit).astype(held_as)


def setup_inputs(seed: int = 0) -> dict:
    key_of = jax.random.split(jax.random.key(seed), 4)
    source = draw_source(jax.random.fold_in(key_of[3], 71), 0)
    aux_field = normal_values(key_of[1], (SLICES, SITES), 0.4, 2.0, ((0, 4), (1, 8)), jnp.float32)
    hopping_exp = draw_hopping_exp(jax.random.fold_in(key_of[3], 71), 0)
    return {"source": source, "aux_field": aux_field, "hopping_exp": hopping_exp}


def apply_kernel(field, hopping_exp):
    return jnp.einsum("trc,sc->trs", field, hopping_exp, precision=lax.Precision.HIGHEST)


def forward_apply(field, boost, hopping_exp):
    image = apply_kernel(field, hopping_exp)
    shifted = jnp.concatenate([-image[-1:], image[:-1]], axis=0)
    return field - boost[:, None, :] * shifted


def adjoint_apply(field, boost, hopping_exp):
    image = apply_kernel(boost[:, None, :] * field, hopping_exp)
    shifted = jnp.concatenate([image[1:], -image[:1]], axis=0)
    return field - shifted


def reference(source, aux_field, hopping_exp):
    boost = jnp.exp(aux_field)
    solution_field = jnp.zeros_like(source)
    residual = source
    direction = source
    norm_now = jnp.sum(residual * residual, axis=(0, 2))
    for iteration in range(ITERS):
        image = adjoint_apply(forward_apply(direction, boost, hopping_exp), boost, hopping_exp)
        curvature = jnp.sum(direction * image, axis=(0, 2))
        alpha = (norm_now / curvature)[None, :, None]
        solution_field = solution_field + alpha * direction
        residual = residual - alpha * image
        if iteration + 1 < ITERS:
            norm_next = jnp.sum(residual * residual, axis=(0, 2))
            direction = residual + (norm_next / norm_now)[None, :, None] * direction
            norm_now = norm_next
    return solution_field, residual
```

```python
import functools

import jax
import jax.numpy as jnp
from jax import lax
from jax.experimental import pallas as pl
from jax.experimental.pallas import tpu as pltpu
from jax.sharding import PartitionSpec as P

ITERS = 2


def passed_along(block, axis, distance):
    devices = range(lax.axis_size(axis))
    route = [((i - distance) % len(devices), i) for i in devices]
    return lax.ppermute(block, axis, route)


def kernel_fold(column_major, piece):
    return jnp.einsum("trc,cs->trs", piece, column_major, precision=lax.Precision.HIGHEST)


def forward_kernel(field, column_major):
    return kernel_fold(column_major, lax.all_gather(field, "site", axis=2, tiled=True))


def adjoint_kernel(field, column_major):
    return kernel_fold(column_major, lax.all_gather(field, "site", axis=2, tiled=True))


def forward_apply(field, boost, column_major):
    tm_index = lax.axis_index("tm")
    image = forward_kernel(field, column_major)
    prior = passed_along(image[-1], "tm", 1)
    prior = jnp.where(tm_index == 0, -prior, prior)
    shifted = jnp.concatenate([prior[None], image[:-1]], axis=0)
    return field - boost[:, None, :] * shifted


def adjoint_apply(field, boost, column_major):
    tm_index = lax.axis_index("tm")
    last_index = lax.axis_size("tm") - 1
    boosted = boost[:, None, :] * field
    image = adjoint_kernel(boosted, column_major)
    following = passed_along(image[0], "tm", -1)
    following = jnp.where(tm_index == last_index, -following, following)
    shifted = jnp.concatenate([image[1:], following[None]], axis=0)
    return field - shifted


def plain_solve(source, aux_field, hopping_exp):
    column_major = jnp.transpose(hopping_exp)
    boost = jnp.exp(aux_field)
    solution_field = jnp.zeros_like(source)
    residual = source
    direction = source
    norm_now = lax.psum(jnp.sum(residual * residual, axis=(0, 2)), ("tm", "site"))
    for iteration in range(ITERS):
        forward = forward_apply(direction, boost, column_major)
        image = adjoint_apply(forward, boost, column_major)
        curvature = lax.psum(jnp.sum(direction * image, axis=(0, 2)), ("tm", "site"))
        alpha = (norm_now / curvature)[None, :, None]
        solution_field = solution_field + alpha * direction
        residual = residual - alpha * image
        if iteration + 1 < ITERS:
            norm_next = lax.psum(jnp.sum(residual * residual, axis=(0, 2)), ("tm", "site"))
            direction = residual + (norm_next / norm_now)[None, :, None] * direction
            norm_now = norm_next
    return (solution_field, residual)


MESH = pl.DeviceIdType.MESH
TRANSPOSED = (((1,), (1,)), ((), ()))
LANES = 128
APPLIES = 2 * ITERS
SUMS = 3
STAGES = 4


def crossed(index, mask):
    bit = 1
    while bit <= mask:
        if mask & bit:
            index = index + bit - 2 * bit * ((index // bit) % 2)
        bit *= 2
    return index


def lane_sums(block):
    folded = jnp.sum(block * block, axis=0)
    total = folded[:, :LANES]
    for start in range(LANES, folded.shape[1], LANES):
        total = total + folded[:, start : start + LANES]
    return total


def solve_kernel(
    tm_size, n, source, aux, hopping, solution_out, residual_out,
    high, low, stage, held, edge, boost, image_first, residual, direction, tm_sums, site_sums,
    stage_sem, own_send, pass_send, edge_send, recv, tm_send, tm_recv, site_send, site_recv,
):
    slices, rhs, width = source.shape
    tm, site = lax.axis_index("tm"), lax.axis_index("site")
    unwaited = []

    def load(slot):
        first = pl.multiple_of(crossed(site, slot) * width, width)
        return pltpu.make_async_copy(hopping.at[:, pl.ds(first, width)], stage.at[slot % STAGES], stage_sem.at[slot])

    for slot in range(min(STAGES, n)):
        load(slot).start()

    barrier = pltpu.get_barrier_semaphore()
    for mask in range(1, tm_size):
        pl.semaphore_signal(barrier, inc=1, device_id=(crossed(tm, mask), site), device_id_type=MESH)
    for mask in range(1, n):
        pl.semaphore_signal(barrier, inc=1, device_id=(tm, crossed(site, mask)), device_id_type=MESH)

    for t in range(slices):
        boost[t] = jnp.broadcast_to(jnp.exp(aux[t : t + 1, :]), (rhs, width))

    pl.semaphore_wait(barrier, tm_size - 1 + n - 1)

    def send(src, dst, send_sem, recv_sem, device):
        copy = pltpu.make_async_remote_copy(
            src_ref=src, dst_ref=dst, send_sem=send_sem, recv_sem=recv_sem, device_id=device, device_id_type=MESH
        )
        copy.start()
        unwaited.append(copy)

    def arrived(ref, sem):
        pltpu.make_async_copy(ref, ref, sem).wait()

    def sum_rows(which):
        return pl.ds(0, 2 * rhs if which == 0 else rhs)

    def sum_over_tm(which):
        rows = sum_rows(which)
        for mask in range(1, tm_size):
            send(tm_sums.at[which, 0, rows], tm_sums.at[which, mask, rows], tm_send.at[which, mask],
                 tm_recv.at[which, mask], (crossed(tm, mask), site))

    def sum_over_site(which):
        rows = sum_rows(which)
        total = tm_sums[which, 0, rows]
        for mask in range(1, tm_size):
            arrived(tm_sums.at[which, mask, rows], tm_recv.at[which, mask])
            total = total + tm_sums[which, mask, rows]
        site_sums[which, 0, rows] = total
        for mask in range(1, n):
            send(site_sums.at[which, 0, rows], site_sums.at[which, mask, rows], site_send.at[which, mask],
                 site_recv.at[which, mask], (tm, crossed(site, mask)))

    def summed(which):
        rows = sum_rows(which)
        total = site_sums[which, 0, rows]
        for mask in range(1, n):
            arrived(site_sums.at[which, mask, rows], site_recv.at[which, mask])
            total = total + site_sums[which, mask, rows]
        return jnp.sum(total, axis=1, keepdims=True)

    def split(slot):
        load(slot).wait()
        step = width // 8

        @pl.loop(0, width, step=step)
        def _(row):
            rows = pl.ds(pl.multiple_of(row, step), step)
            value = stage[slot % STAGES, rows, :]
            upper = value.astype(jnp.bfloat16)
            high[slot, rows, :] = upper
            low[slot, rows, :] = (value - upper.astype(jnp.float32)).astype(jnp.bfloat16)

        if slot + STAGES < n:
            load(slot + STAGES).start()

    def product(turn, slot):
        value = held[turn, slot].reshape(slices * rhs, width)
        upper = value.astype(jnp.bfloat16)
        lower = (value - upper.astype(jnp.float32)).astype(jnp.bfloat16)
        both = lax.dot_general(
            jnp.concatenate([upper, lower], axis=0), high[slot], TRANSPOSED, preferred_element_type=jnp.float32
        )
        rest = lax.dot_general(upper, low[slot], TRANSPOSED, preferred_element_type=jnp.float32)
        return both[: slices * rhs] + (both[slices * rhs :] + rest)

    def apply(turn, field, pending):
        forward = turn % 2 == 0
        own = pl.ds(1 if forward else 0, slices - 1)
        far = pl.ds(0 if forward else slices - 1, 1)
        if forward:
            edge[turn] = field[slices - 1 :]
            held[turn, 0, own] = field[: slices - 1]
            target = lax.rem(tm + 1, tm_size)
        else:
            edge[turn] = field[:1]
            held[turn, 0, own] = field[1:]
            target = lax.rem(tm + tm_size - 1, tm_size)
        send(edge.at[turn], held.at[turn, 0, far], edge_send.at[turn], recv.at[turn, 1, 0], (target, site))
        near = [1] + list(range(2, n, 2))

        def spread(part, which):
            for slot in near:
                send(held.at[turn, 0, part], held.at[turn, slot, part], own_send.at[turn, which, slot],
                     recv.at[turn, which, slot], (tm, crossed(site, slot)))

        spread(own, 0)
        if pending is not None:
            sum_over_tm(pending)
        if turn == 0:
            split(0)
        arrived(held.at[turn, 0, far], recv.at[turn, 1, 0])
        spread(far, 1)
        total = product(turn, 0)
        for position, slot in enumerate(near + list(range(3, n, 2))):
            if turn == 0:
                split(slot)
            for which, part in ((0, own), (1, far)):
                arrived(held.at[turn, slot, part], recv.at[turn, which, slot])
                if slot % 2 == 0:
                    send(held.at[turn, slot, part], held.at[turn, slot + 1, part], pass_send.at[turn, which, slot],
                         recv.at[turn, which, slot + 1], (tm, crossed(site, 1)))
            if position == 1 and pending is not None:
                sum_over_site(pending)
            total = total + product(turn, slot)
        shifted = total.reshape(slices, rhs, width)
        sign = jnp.where(tm == (0 if forward else tm_size - 1), -1.0, 1.0).astype(jnp.float32)
        if forward:
            return jnp.concatenate([sign * shifted[:1], shifted[1:]], axis=0)
        return jnp.concatenate([shifted[: slices - 1], sign * shifted[slices - 1 :]], axis=0)

    first = source[...] - boost[...] * apply(0, source[...], None)
    image_first[...] = first
    tm_sums[0, 0, pl.ds(0, rhs)] = lane_sums(source[...])
    tm_sums[0, 0, pl.ds(rhs, rhs)] = lane_sums(first)

    image = image_first[...] - apply(1, boost[...] * first, 0)
    sums = summed(0)
    norm_now, curvature = sums[:rhs], sums[rhs:]
    alpha = norm_now / curvature
    solution_out[...] = alpha * source[...]
    after = source[...] - alpha * image
    residual[...] = after
    tm_sums[1, 0, pl.ds(0, rhs)] = lane_sums(after)

    second = residual[...] - boost[...] * apply(2, after, 1)
    norm_next = summed(1)
    beta = norm_next / norm_now
    direction[...] = residual[...] + beta * source[...]
    second = second + beta * image_first[...]
    image_first[...] = second
    tm_sums[2, 0, pl.ds(0, rhs)] = lane_sums(second)

    image = image_first[...] - apply(3, boost[...] * second, 2)
    alpha = norm_next / summed(2)
    solution_out[...] = solution_out[...] + alpha * direction[...]
    residual_out[...] = residual[...] - alpha * image

    for copy in unwaited:
        copy.wait_send()


def on_device(source, aux_field, hopping_exp):
    tm_size, n = lax.axis_size("tm"), lax.axis_size("site")
    slices, rhs, width = source.shape
    fits = width % LANES == 0 and n >= 2 and n & (n - 1) == 0 and tm_size >= 2 and tm_size & (tm_size - 1) == 0
    if not fits or slices < 2 or rhs % 8 or ITERS != 2:
        return plain_solve(source, aux_field, hopping_exp)
    field = jax.ShapeDtypeStruct(source.shape, jnp.float32)
    local = pltpu.VMEM(source.shape, jnp.float32)
    dma = pltpu.SemaphoreType.DMA
    whole = pl.BlockSpec(memory_space=pltpu.VMEM)
    return pl.pallas_call(
        functools.partial(solve_kernel, tm_size, n),
        out_shape=(field, field),
        in_specs=[whole, whole, pl.BlockSpec(memory_space=pl.ANY)],
        out_specs=(whole, whole),
        scratch_shapes=[
            pltpu.VMEM((n, width, width), jnp.bfloat16),
            pltpu.VMEM((n, width, width), jnp.bfloat16),
            pltpu.VMEM((STAGES, width, width), jnp.float32),
            pltpu.VMEM((APPLIES, n, slices, rhs, width), jnp.float32),
            pltpu.VMEM((APPLIES, 1, rhs, width), jnp.float32),
            local,
            local,
            local,
            local,
            pltpu.VMEM((SUMS, tm_size, 2 * rhs, LANES), jnp.float32),
            pltpu.VMEM((SUMS, n, 2 * rhs, LANES), jnp.float32),
            dma((n,)),
            dma((APPLIES, 2, n)),
            dma((APPLIES, 2, n)),
            dma((APPLIES,)),
            dma((APPLIES, 2, n)),
            dma((SUMS, tm_size)),
            dma((SUMS, tm_size)),
            dma((SUMS, n)),
            dma((SUMS, n)),
        ],
        compiler_params=pltpu.CompilerParams(
            collective_id=0, has_side_effects=True, vmem_limit_bytes=52 * 1024 * 1024
        ),
        cost_estimate=pl.CostEstimate(
            flops=APPLIES * 6 * slices * rhs * n * width * width,
            bytes_accessed=4 * n * width * width,
            transcendentals=slices * width,
        ),
        name="conjugate_gradient",
    )(source, aux_field, hopping_exp)


def solution(mesh):
    placed = (P("tm", None, "site"), P("tm", "site"), P("site", None))
    return jax.shard_map(
        on_device,
        mesh=mesh,
        in_specs=placed,
        out_specs=(P("tm", None, "site"), P("tm", None, "site")),
        check_vma=False,
    )
```

```python
import functools

import jax
import jax.numpy as jnp
from jax import lax
from jax.experimental import pallas as pl
from jax.experimental.pallas import tpu as pltpu
from jax.sharding import PartitionSpec as P

ITERS = 2


def passed_along(block, axis, distance):
    devices = range(lax.axis_size(axis))
    route = [((i - distance) % len(devices), i) for i in devices]
    return lax.ppermute(block, axis, route)


def kernel_fold(column_major, piece):
    return jnp.einsum("trc,cs->trs", piece, column_major, precision=lax.Precision.HIGHEST)


def forward_kernel(field, column_major):
    return kernel_fold(column_major, lax.all_gather(field, "site", axis=2, tiled=True))


def adjoint_kernel(field, column_major):
    return kernel_fold(column_major, lax.all_gather(field, "site", axis=2, tiled=True))


def forward_apply(field, boost, column_major):
    tm_index = lax.axis_index("tm")
    image = forward_kernel(field, column_major)
    prior = passed_along(image[-1], "tm", 1)
    prior = jnp.where(tm_index == 0, -prior, prior)
    shifted = jnp.concatenate([prior[None], image[:-1]], axis=0)
    return field - boost[:, None, :] * shifted


def adjoint_apply(field, boost, column_major):
    tm_index = lax.axis_index("tm")
    last_index = lax.axis_size("tm") - 1
    boosted = boost[:, None, :] * field
    image = adjoint_kernel(boosted, column_major)
    following = passed_along(image[0], "tm", -1)
    following = jnp.where(tm_index == last_index, -following, following)
    shifted = jnp.concatenate([image[1:], following[None]], axis=0)
    return field - shifted


def plain_solve(source, aux_field, hopping_exp):
    column_major = jnp.transpose(hopping_exp)
    boost = jnp.exp(aux_field)
    solution_field = jnp.zeros_like(source)
    residual = source
    direction = source
    norm_now = lax.psum(jnp.sum(residual * residual, axis=(0, 2)), ("tm", "site"))
    for iteration in range(ITERS):
        forward = forward_apply(direction, boost, column_major)
        image = adjoint_apply(forward, boost, column_major)
        curvature = lax.psum(jnp.sum(direction * image, axis=(0, 2)), ("tm", "site"))
        alpha = (norm_now / curvature)[None, :, None]
        solution_field = solution_field + alpha * direction
        residual = residual - alpha * image
        if iteration + 1 < ITERS:
            norm_next = lax.psum(jnp.sum(residual * residual, axis=(0, 2)), ("tm", "site"))
            direction = residual + (norm_next / norm_now)[None, :, None] * direction
            norm_now = norm_next
    return (solution_field, residual)


MESH = pl.DeviceIdType.MESH
PLAIN = (((1,), (0,)), ((), ()))
LANES = 128
APPLIES = 2 * ITERS
SUMS = 3
STAGES = 4


def crossed(index, mask):
    bit = 1
    while bit <= mask:
        if mask & bit:
            index = index + bit - 2 * bit * ((index // bit) % 2)
        bit *= 2
    return index


def lane_sums(block):
    folded = jnp.sum(block * block, axis=0)
    total = folded[:, :LANES]
    for start in range(LANES, folded.shape[1], LANES):
        total = total + folded[:, start : start + LANES]
    return total


def solve_kernel(
    tm_size, n, source, aux, hopping, solution_out, residual_out,
    high, low, stage, held, edge, boost, image_first, residual, direction, tm_sums, site_sums,
    stage_sem, own_send, pass_send, edge_send, recv, tm_send, tm_recv, site_send, site_recv,
):
    slices, rhs, width = source.shape
    tm, site = lax.axis_index("tm"), lax.axis_index("site")
    unwaited = []

    def load(slot):
        first = pl.multiple_of(crossed(site, slot) * width, width)
        return pltpu.make_async_copy(hopping.at[:, pl.ds(first, width)], stage.at[slot % STAGES], stage_sem.at[slot])

    for slot in range(min(STAGES, n)):
        load(slot).start()

    barrier = pltpu.get_barrier_semaphore()
    for mask in range(1, tm_size):
        pl.semaphore_signal(barrier, inc=1, device_id=(crossed(tm, mask), site), device_id_type=MESH)
    for mask in range(1, n):
        pl.semaphore_signal(barrier, inc=1, device_id=(tm, crossed(site, mask)), device_id_type=MESH)

    for t in range(slices):
        boost[t] = jnp.broadcast_to(jnp.exp(aux[t : t + 1, :]), (rhs, width))

    pl.semaphore_wait(barrier, tm_size - 1 + n - 1)

    def send(src, dst, send_sem, recv_sem, device):
        copy = pltpu.make_async_remote_copy(
            src_ref=src, dst_ref=dst, send_sem=send_sem, recv_sem=recv_sem, device_id=device, device_id_type=MESH
        )
        copy.start()
        unwaited.append(copy)

    def arrived(ref, sem):
        pltpu.make_async_copy(ref, ref, sem).wait()

    def sum_rows(which):
        return pl.ds(0, 2 * rhs if which == 0 else rhs)

    def sum_over_tm(which):
        rows = sum_rows(which)
        for mask in range(1, tm_size):
            send(tm_sums.at[which, 0, rows], tm_sums.at[which, mask, rows], tm_send.at[which, mask],
                 tm_recv.at[which, mask], (crossed(tm, mask), site))

    def sum_over_site(which):
        rows = sum_rows(which)
        total = tm_sums[which, 0, rows]
        for mask in range(1, tm_size):
            arrived(tm_sums.at[which, mask, rows], tm_recv.at[which, mask])
            total = total + tm_sums[which, mask, rows]
        site_sums[which, 0, rows] = total
        for mask in range(1, n):
            send(site_sums.at[which, 0, rows], site_sums.at[which, mask, rows], site_send.at[which, mask],
                 site_recv.at[which, mask], (tm, crossed(site, mask)))

    def summed(which):
        rows = sum_rows(which)
        total = site_sums[which, 0, rows]
        for mask in range(1, n):
            arrived(site_sums.at[which, mask, rows], site_recv.at[which, mask])
            total = total + site_sums[which, mask, rows]
        return jnp.sum(total, axis=1, keepdims=True)

    def split(slot):
        load(slot).wait()
        step = LANES

        @pl.loop(0, width, step=step)
        def _(row):
            rows = pl.ds(pl.multiple_of(row, step), step)
            value = jnp.transpose(stage[slot % STAGES, :, rows])
            upper = value.astype(jnp.bfloat16)
            high[slot, rows, :] = upper
            low[slot, rows, :] = (value - upper.astype(jnp.float32)).astype(jnp.bfloat16)

        if slot + STAGES < n:
            load(slot + STAGES).start()

    def product(turn, slot):
        value = held[turn, slot].reshape(slices * rhs, width)
        upper = value.astype(jnp.bfloat16)
        lower = (value - upper.astype(jnp.float32)).astype(jnp.bfloat16)
        both = lax.dot_general(
            jnp.concatenate([upper, lower], axis=0), high[slot], PLAIN, preferred_element_type=jnp.float32
        )
        rest = lax.dot_general(upper, low[slot], PLAIN, preferred_element_type=jnp.float32)
        return both[: slices * rhs] + (both[slices * rhs :] + rest)

    def apply(turn, field, pending):
        forward = turn % 2 == 0
        own = pl.ds(1 if forward else 0, slices - 1)
        far = pl.ds(0 if forward else slices - 1, 1)
        if forward:
            edge[turn] = field[slices - 1 :]
            held[turn, 0, own] = field[: slices - 1]
            target = lax.rem(tm + 1, tm_size)
        else:
            edge[turn] = field[:1]
            held[turn, 0, own] = field[1:]
            target = lax.rem(tm + tm_size - 1, tm_size)
        send(edge.at[turn], held.at[turn, 0, far], edge_send.at[turn], recv.at[turn, 1, 0], (target, site))
        near = [1] + list(range(2, n, 2))

        def spread(part, which):
            for slot in near:
                send(held.at[turn, 0, part], held.at[turn, slot, part], own_send.at[turn, which, slot],
                     recv.at[turn, which, slot], (tm, crossed(site, slot)))

        spread(own, 0)
        if pending is not None:
            sum_over_tm(pending)
        if turn == 0:
            split(0)
        arrived(held.at[turn, 0, far], recv.at[turn, 1, 0])
        spread(far, 1)
        total = product(turn, 0)
        for position, slot in enumerate(near + list(range(3, n, 2))):
            if turn == 0:
                split(slot)
            for which, part in ((0, own), (1, far)):
                arrived(held.at[turn, slot, part], recv.at[turn, which, slot])
                if slot % 2 == 0:
                    send(held.at[turn, slot, part], held.at[turn, slot + 1, part], pass_send.at[turn, which, slot],
                         recv.at[turn, which, slot + 1], (tm, crossed(site, 1)))
            if position == 1 and pending is not None:
                sum_over_site(pending)
            total = total + product(turn, slot)
        shifted = total.reshape(slices, rhs, width)
        sign = jnp.where(tm == (0 if forward else tm_size - 1), -1.0, 1.0).astype(jnp.float32)
        if forward:
            return jnp.concatenate([sign * shifted[:1], shifted[1:]], axis=0)
        return jnp.concatenate([shifted[: slices - 1], sign * shifted[slices - 1 :]], axis=0)

    first = source[...] - boost[...] * apply(0, source[...], None)
    image_first[...] = first
    tm_sums[0, 0, pl.ds(0, rhs)] = lane_sums(source[...])
    tm_sums[0, 0, pl.ds(rhs, rhs)] = lane_sums(first)

    image = image_first[...] - apply(1, boost[...] * first, 0)
    sums = summed(0)
    norm_now, curvature = sums[:rhs], sums[rhs:]
    alpha = norm_now / curvature
    solution_out[...] = alpha * source[...]
    after = source[...] - alpha * image
    residual[...] = after
    tm_sums[1, 0, pl.ds(0, rhs)] = lane_sums(after)

    second = residual[...] - boost[...] * apply(2, after, 1)
    norm_next = summed(1)
    beta = norm_next / norm_now
    direction[...] = residual[...] + beta * source[...]
    second = second + beta * image_first[...]
    image_first[...] = second
    tm_sums[2, 0, pl.ds(0, rhs)] = lane_sums(second)

    image = image_first[...] - apply(3, boost[...] * second, 2)
    alpha = norm_next / summed(2)
    solution_out[...] = solution_out[...] + alpha * direction[...]
    residual_out[...] = residual[...] - alpha * image

    for copy in unwaited:
        copy.wait_send()


def on_device(source, aux_field, hopping_exp):
    tm_size, n = lax.axis_size("tm"), lax.axis_size("site")
    slices, rhs, width = source.shape
    fits = width % LANES == 0 and n >= 2 and n & (n - 1) == 0 and tm_size >= 2 and tm_size & (tm_size - 1) == 0
    if not fits or slices < 2 or rhs % 8 or ITERS != 2:
        return plain_solve(source, aux_field, hopping_exp)
    field = jax.ShapeDtypeStruct(source.shape, jnp.float32)
    local = pltpu.VMEM(source.shape, jnp.float32)
    dma = pltpu.SemaphoreType.DMA
    whole = pl.BlockSpec(memory_space=pltpu.VMEM)
    return pl.pallas_call(
        functools.partial(solve_kernel, tm_size, n),
        out_shape=(field, field),
        in_specs=[whole, whole, pl.BlockSpec(memory_space=pl.ANY)],
        out_specs=(whole, whole),
        scratch_shapes=[
            pltpu.VMEM((n, width, width), jnp.bfloat16),
            pltpu.VMEM((n, width, width), jnp.bfloat16),
            pltpu.VMEM((STAGES, width, width), jnp.float32),
            pltpu.VMEM((APPLIES, n, slices, rhs, width), jnp.float32),
            pltpu.VMEM((APPLIES, 1, rhs, width), jnp.float32),
            local,
            local,
            local,
            local,
            pltpu.VMEM((SUMS, tm_size, 2 * rhs, LANES), jnp.float32),
            pltpu.VMEM((SUMS, n, 2 * rhs, LANES), jnp.float32),
            dma((n,)),
            dma((APPLIES, 2, n)),
            dma((APPLIES, 2, n)),
            dma((APPLIES,)),
            dma((APPLIES, 2, n)),
            dma((SUMS, tm_size)),
            dma((SUMS, tm_size)),
            dma((SUMS, n)),
            dma((SUMS, n)),
        ],
        compiler_params=pltpu.CompilerParams(
            collective_id=0, has_side_effects=True, vmem_limit_bytes=52 * 1024 * 1024
        ),
        cost_estimate=pl.CostEstimate(
            flops=APPLIES * 6 * slices * rhs * n * width * width,
            bytes_accessed=4 * n * width * width,
            transcendentals=slices * width,
        ),
        name="conjugate_gradient",
    )(source, aux_field, hopping_exp)


def solution(mesh):
    placed = (P("tm", None, "site"), P("tm", "site"), P("site", None))
    return jax.shard_map(
        on_device,
        mesh=mesh,
        in_specs=placed,
        out_specs=(P("tm", None, "site"), P("tm", None, "site")),
        check_vma=False,
    )
```
